32 devices in a mesh: level: 8 (over z, x), slab: 4 (over y, core).
Axes of the slice: x: 2, y: 2, z: 4, core: 2. Of those that a mesh axis runs over, the one named last changes fastest.
Arguments:
- trajectory: float32 [8, 8, 8, 32, 128], P('level', None, 'slab'), may hold values from -6 to 6
- first_latent: float32 [8, 8, 32, 128], P(None, 'slab'), may hold values from -6 to 6
- noise_draw: float32 [8, 8, 8, 32, 128], P('level', None, 'slab'), may hold values from -6 to 6
- w_in: bfloat16 [64, 8, 3, 3, 3], replicated, may hold values from -0.4375 to 0.4375
- bias_in: float32 [64], replicated, may hold values from -3 to 3
- level_bias: float32 [8, 64], P('level'), may hold values from -3 to 3
- w_out: bfloat16 [8, 64, 3, 3, 3], replicated, may hold values from -0.15625 to 0.15625
- bias_out: float32 [8], replicated, may hold values from -2 to 2
- drift_coef: float32 [8], P('level'), may hold values from -0.12 to -0.02
- eps_coef: float32 [8], P('level'), may hold values from 0.05 to 0.3
- noise_coef: float32 [8], P('level'), may hold values from 0.05 to 0.2
Outputs:
- next_states: float32 [8, 8, 8, 32, 128], P('level', None, 'slab')
The draws below stay inside these ranges and needn't reach their ends.
All inputs are finite; a program needn't handle non-finite values.
Results may differ from the reference program's by a relative error of at most 0.0016.
Values may be sent and summed in bfloat16 or wider, within the bound.
A program may use at most 64 MiB of HBM per device.

```python
import math
import jax
import jax.numpy as jnp
from jax import lax

C = 8
HID = 64
H = 32
W = 128
ITERS = 2
LEVELS = 8
NZ = 8


def block_scale(own_key, dims, shards, smallest, top_value):
    def one(dim, shards_of):
        draws = jax.random.uniform(jax.random.fold_in(jax.random.fold_in(own_key, 6), dim), (shards_of,), jnp.float32, smallest / len(shards), top_value / len(shards))
        return jnp.repeat(jnp.exp(draws), dims[dim] // shards_of).reshape((-1,) + (1,) * (len(dims) - dim - 1))

    level = one(*shards[0])
    for cut in shards[1:]:
        level = level * one(*cut)
    return level


def gaussian(key, extent, spread, most, cuts=(), held_as=jnp.bfloat16):
    values = spread * jax.random.normal(key, extent, jnp.float32)
    if cuts:
        values = values * block_scale(key, extent, cuts, -0.22, 0.18)
    return jnp.clip(values, -most, most).astype(held_as)


def setup_inputs(seed: int = 0) -> dict:
    key_list = jax.random.split(jax.random.key(seed), 12)
    return {
        "trajectory": gaussian(key_list[0], (LEVELS, C, NZ, H, W), 1.0, 6.0, ((0, 8), (2, 4)), jnp.float32),
        "first_latent": gaussian(key_list[1], (C, NZ, H, W), 1.0, 6.0, ((1, 4),), jnp.float32),
        "noise_draw": gaussian(key_list[2], (LEVELS, C, NZ, H, W), 1.0, 6.0, ((0, 8), (2, 4)), jnp.float32),
        "w_in": gaussian(key_list[3], (HID, C, 3, 3, 3), (C * 27) ** -0.5, 0.4375),
        "bias_in": gaussian(key_list[4], (HID,), 0.5, 3.0, (), jnp.float32),
        "level_bias": gaussian(key_list[5], (LEVELS, HID), 0.5, 3.0, ((0, 8),), jnp.float32),
        "w_out": gaussian(key_list[6], (C, HID, 3, 3, 3), (HID * 27) ** -0.5, 0.15625),
        "bias_out": gaussian(key_list[7], (C,), 0.3, 2.0, (), jnp.float32),
        "drift_coef": jnp.clip(-0.12 + 0.09999999776482582 * jax.random.uniform(key_list[8], (LEVELS,), jnp.float32) ** block_scale(key_list[8], (LEVELS,), ((0, 8),), -0.2, 0.2), -0.12, -0.02),
        "eps_coef": jnp.clip(jnp.exp(math.log(0.3) - 1.7917595 * jax.random.uniform(key_list[9], (LEVELS,), jnp.float32) ** block_scale(key_list[9], (LEVELS,), ((0, 8),), -0.2, 0.2)), 0.05, 0.3),
        "noise_coef": jnp.clip(jnp.exp(math.log(0.2) - 1.3862944 * jax.random.uniform(key_list[10], (LEVELS,), jnp.float32) ** block_scale(key_list[10], (LEVELS,), ((0, 8),), -0.2, 0.2)), 0.05, 0.2),
    }


def convolve(field, kernel):
    return lax.conv_general_dilated(field[None].astype(jnp.float32), kernel.astype(jnp.float32), (1, 1, 1), ((1, 1), (1, 1), (1, 1)), dimension_numbers=("NCDHW", "OIDHW", "NCDHW"), precision=lax.Precision.HIGHEST)[0]


def reference(trajectory, first_latent, noise_draw, w_in, bias_in, level_bias, w_out, bias_out, drift_coef, eps_coef, noise_coef):
    def level_step(items):
        current, fresh, level_row, drift, scale_eps, scale_noise = items
        latent_bf = current.astype(jnp.bfloat16)
        before = convolve(latent_bf, w_in)
        hidden = jax.nn.silu(before + (bias_in + level_row)[:, None, None, None]).astype(jnp.bfloat16)
        predicted = convolve(hidden, w_out) + bias_out[:, None, None, None]
        return drift * current + scale_eps * predicted + scale_noise * fresh

    states = trajectory
    result = trajectory
    for step in range(ITERS):
        increment = lax.map(level_step, (states, noise_draw, level_bias, drift_coef, eps_coef, noise_coef))
        inclusive = jnp.cumsum(increment, axis=0)
        if step + 1 < ITERS:
            shifted = jnp.concatenate([jnp.zeros_like(inclusive[:1]), inclusive[:-1]], axis=0)
            states = first_latent[None] + shifted
        else:
            result = first_latent[None] + inclusive
    return result
```

```python
import functools

import jax
import jax.numpy as jnp
from jax import lax
from jax.experimental import pallas as pl
from jax.experimental.pallas import tpu as pltpu
from jax.sharding import PartitionSpec as P

ITERS = 2
MESH = pl.DeviceIdType.MESH
F32 = jnp.float32
BF16 = jnp.bfloat16


def kernel(
    dims,
    traj, first, noise, w_in, bias_in, level_bias, w_out, bias_out, drift, eps, nco,
    out,
    a1, a2, bias_col, cur, base, xs, y, inc, sb, hl, hr, xsb, xr, zsb, zr, xr_last, zsb_last, zr_last,
    hs_sem, hr_sem, x_ssem, x_rsem, z_ssem, z_rsem,
):
    chans, hid, depth, rows, width, levels, slabs, chunk, block = dims
    level, slab = lax.axis_index("level"), lax.axis_index("slab")
    odd = lax.rem(level, 2)
    group = lax.div(level, 2)
    groups = levels // 2
    partner = level + 1 - 2 * odd
    stride = depth * rows
    own = depth * chans
    side = 2 * chans
    full = depth + 4
    mid = depth + 2
    chunks = rows // chunk
    lanes = lax.broadcasted_iota(jnp.int32, (1, width), 1)
    not_first = lanes > 0
    not_last = lanes < width - 1

    barrier = pltpu.get_barrier_semaphore()
    pl.semaphore_signal(barrier, inc=1, device_id={"level": partner}, device_id_type=MESH)

    @pl.when(group > 0)
    def _():
        pl.semaphore_signal(barrier, inc=1, device_id={"level": level - 2}, device_id_type=MESH)

    @pl.when(group < groups - 1)
    def _():
        pl.semaphore_signal(barrier, inc=1, device_id={"level": level + 2}, device_id_type=MESH)

    @pl.when(slab > 0)
    def _():
        pl.semaphore_signal(barrier, inc=1, device_id={"slab": slab - 1}, device_id_type=MESH)

    @pl.when(slab < slabs - 1)
    def _():
        pl.semaphore_signal(barrier, inc=1, device_id={"slab": slab + 1}, device_id_type=MESH)

    def one(cond):
        return jnp.where(cond, 1, 0)

    def rows_of(ref, h):
        return jnp.concatenate(
            [ref[pl.ds(d * rows + h, chans, stride=stride), :] for d in range(depth)], axis=0
        )

    def at(h, n=1, pad=0):
        return pl.ds(pl.multiple_of((h + pad) * width, width), n * width)

    @pl.loop(0, chunks)
    def _(j):
        for r in range(chunk):
            h = j * chunk + r
            v = rows_of(traj, h)
            cur[:, at(h)] = v
            sb[0, :, at(h)] = v.astype(BF16)

    pl.semaphore_wait(
        barrier,
        1 + one(group > 0) + one(group < groups - 1) + one(slab > 0) + one(slab < slabs - 1),
    )

    def halo_copies(it, j, span):
        to_right = pltpu.make_async_remote_copy(
            src_ref=sb.at[it, pl.ds(own - side, side), span],
            dst_ref=hl.at[it, :, span],
            send_sem=hs_sem.at[it, 0, j],
            recv_sem=hr_sem.at[it, 0, j],
            device_id={"slab": slab + 1},
            device_id_type=MESH,
        )
        to_left = pltpu.make_async_remote_copy(
            src_ref=sb.at[it, pl.ds(0, side), span],
            dst_ref=hr.at[it, :, span],
            send_sem=hs_sem.at[it, 1, j],
            recv_sem=hr_sem.at[it, 1, j],
            device_id={"slab": slab - 1},
            device_id_type=MESH,
        )
        return to_right, to_left

    def halo_start(it, j):
        to_right, to_left = halo_copies(it, j, at(j * chunk, chunk))

        @pl.when(slab < slabs - 1)
        def _():
            to_right.start()

        @pl.when(slab > 0)
        def _():
            to_left.start()

    def halo_recv(it, j):
        to_right, to_left = halo_copies(it, j, at(j * chunk, chunk))

        @pl.when(slab > 0)
        def _():
            to_right.wait_recv()

        @pl.when(slab < slabs - 1)
        def _():
            to_left.wait_recv()

    def halo_sent(it, j):
        to_right, to_left = halo_copies(it, j, at(j * chunk, chunk))

        @pl.when(slab < slabs - 1)
        def _():
            to_right.wait_send()

        @pl.when(slab > 0)
        def _():
            to_left.wait_send()

    def wires(it):
        if it == ITERS - 1:
            return inc, xr_last, zsb_last, zr_last
        return xsb.at[it], xr.at[it], zsb.at[it], zr.at[it]

    def pair_copy(it, j):
        span = at(j * chunk, chunk)
        src, dst, _, _ = wires(it)
        return pltpu.make_async_remote_copy(
            src_ref=src.at[:, span],
            dst_ref=dst.at[:, span],
            send_sem=x_ssem.at[it, j],
            recv_sem=x_rsem.at[it, j],
            device_id={"level": partner},
            device_id_type=MESH,
        )

    def chain_copy(it, j):
        span = at(j * chunk, chunk)
        _, _, src, dst = wires(it)
        return pltpu.make_async_remote_copy(
            src_ref=src.at[:, span],
            dst_ref=dst.at[:, span],
            send_sem=z_ssem.at[it, j],
            recv_sem=z_rsem.at[it, j],
            device_id={"level": level + 2},
            device_id_type=MESH,
        )

    @pl.loop(0, chunks)
    def _(j):
        halo_start(0, j)

    @pl.when(slab == 0)
    def _():
        hl[...] = jnp.zeros_like(hl)

    @pl.when(slab == slabs - 1)
    def _():
        hr[...] = jnp.zeros_like(hr)

    @pl.when(group == 0)
    def _():
        zr[...] = jnp.zeros_like(zr)
        zr_last[...] = jnp.zeros_like(zr_last)

    for ref, dtype in ((xs, BF16), (y, F32)):
        n = ref.shape[0]
        ref[:, 0:width] = jnp.zeros((n, width), dtype)
        ref[:, (rows + 1) * width:(rows + 2) * width] = jnp.zeros((n, width), dtype)

    def tap(ref, n, kd, kh, kw):
        row = ((kd * 3 + kh) * 3 + kw) * n
        return ref[row:row + n, :]

    w_in, w_out = w_in[...].astype(F32), w_out[...].astype(F32)
    zero = jnp.zeros((chans, hid), F32)
    parts = []
    for kh in range(3):
        for kw in range(3):
            for q in range(full):
                parts.append(jnp.concatenate(
                    [tap(w_in, chans, q - p, kh, kw) if 0 <= q - p < 3 else zero for p in range(mid)],
                    axis=1,
                ))
    a1[...] = (0.5 * jnp.concatenate(parts, axis=0)).T.astype(BF16)

    keep = [jnp.float32(1.0)] * mid
    keep[0] = jnp.where(slab > 0, 1.0, 0.0).astype(F32)
    keep[-1] = jnp.where(slab < slabs - 1, 1.0, 0.0).astype(F32)
    parts = []
    for kh in range(3):
        for kw in range(3):
            for d in range(depth):
                parts.append(jnp.concatenate(
                    [tap(w_out, chans, p - d, kh, kw) * keep[p] if 0 <= p - d < 3 else zero for p in range(mid)],
                    axis=1,
                ))
    a2[...] = jnp.concatenate(parts, axis=0).astype(BF16)

    shift = jnp.broadcast_to(0.5 * (bias_in[...] + level_bias[...]), (width, hid)).T
    bias_col[...] = jnp.concatenate([shift] * mid, axis=0)
    tail = jnp.broadcast_to(bias_out[...] * eps[0], (width, chans)).T
    tail = jnp.concatenate([tail] * depth, axis=0)

    @pl.loop(0, chunks)
    def _(j):
        for r in range(chunk):
            h = j * chunk + r
            base[:, at(h)] = rows_of(noise, h) * nco[0] + tail

    drift_v, eps_v = drift[0], eps[0]

    for it in range(ITERS):
        last = it == ITERS - 1
        _, pair_in, chain_out, chain_in = wires(it)

        @pl.loop(0, chunks)
        def _(j):
            halo_recv(it, j)
            for r in range(chunk):
                h = j * chunk + r
                v = jnp.concatenate(
                    [hl[it, :, at(h)], sb[it, :, at(h)], hr[it, :, at(h)]], axis=0
                ).astype(F32)
                n = full * chans
                xs[0:n, at(h, pad=1)] = jnp.where(not_first, pltpu.roll(v, 1, 1), 0.0).astype(BF16)
                xs[n:2 * n, at(h, pad=1)] = v.astype(BF16)
                xs[2 * n:3 * n, at(h, pad=1)] = jnp.where(
                    not_last, pltpu.roll(v, width - 1, 1), 0.0).astype(BF16)

        @pl.loop(0, rows // block)
        def _(b):
            h = b * block
            field = jnp.concatenate([xs[:, at(h, block, kh)] for kh in range(3)], axis=0)
            u = jnp.dot(a1[...], field, preferred_element_type=F32)
            u = u + jnp.concatenate([bias_col[...]] * block, axis=1)
            hidden = (u + u * jnp.tanh(u)).astype(BF16)
            y[:, at(h, block, 1)] = jnp.dot(a2[...], hidden, preferred_element_type=F32)

        @pl.loop(0, chunks)
        def _(j):
            for r in range(chunk):
                h = j * chunk + r
                taps = []
                for kw in range(3):
                    acc = None
                    for kh in range(3):
                        row = (kh * 3 + kw) * own
                        v = y[row:row + own, at(h, pad=kh)]
                        acc = v if acc is None else acc + v
                    taps.append(acc)
                pred = taps[1] + jnp.where(not_first, pltpu.roll(taps[0], 1, 1), 0.0)
                pred = pred + jnp.where(not_last, pltpu.roll(taps[2], width - 1, 1), 0.0)
                v = drift_v * cur[:, at(h)] + (eps_v * pred + base[:, at(h)])
                inc[:, at(h)] = v
                if not last:
                    xsb[it, :, at(h)] = v.astype(BF16)
            pair_copy(it, j).start()

        @pl.loop(0, chunks)
        def _(j):
            pair_copy(it, j).wait_recv()

            @pl.when(group > 0)
            def _():
                chain_copy(it, j).wait_recv()

            span = at(j * chunk, chunk)

            @pl.when(group < groups - 1)
            def _():
                total = chain_in[:, span].astype(F32) + (inc[:, span] + pair_in[:, span].astype(F32))
                chain_out[:, span] = total.astype(chain_out.dtype)
                chain_copy(it, j).start()

            odd_f = odd.astype(F32)
            for r in range(chunk):
                h = j * chunk + r
                v = rows_of(first, h) + (chain_in[:, at(h)].astype(F32) + odd_f * pair_in[:, at(h)].astype(F32))
                if last:
                    v = v + inc[:, at(h)]
                    for d in range(depth):
                        out[pl.ds(d * rows + h, chans, stride=stride), :] = v[d * chans:(d + 1) * chans]
                else:
                    cur[:, at(h)] = v
                    sb[it + 1, :, at(h)] = v.astype(BF16)
            if not last:
                halo_start(it + 1, j)

    @pl.loop(0, chunks)
    def _(j):
        for it in range(ITERS):
            halo_sent(it, j)
            pair_copy(it, j).wait_send()

            @pl.when(group < groups - 1)
            def _():
                chain_copy(it, j).wait_send()


def on_device(levels, slabs, trajectory, first_latent, noise_draw, w_in, bias_in, level_bias,
              w_out, bias_out, drift_coef, eps_coef, noise_coef):
    _, chans, depth, rows, width = trajectory.shape
    hid = w_in.shape[0]
    chunk = 8 if rows % 8 == 0 else rows
    block = 4 if rows % 4 == 0 else rows
    chunks = rows // chunk
    own, side = depth * chans, 2 * chans
    full, mid = depth + 4, depth + 2
    area = rows * width
    padded = (rows + 2) * width
    flat = chans * depth * rows
    dims = (chans, hid, depth, rows, width, levels, slabs, chunk, block)
    vmem = pl.BlockSpec(memory_space=pltpu.VMEM)
    smem = pl.BlockSpec(memory_space=pltpu.SMEM)
    dma = pltpu.SemaphoreType.DMA
    result = pl.pallas_call(
        functools.partial(kernel, dims),
        out_shape=jax.ShapeDtypeStruct((flat, width), F32),
        in_specs=[vmem] * 8 + [smem] * 3,
        out_specs=vmem,
        scratch_shapes=[
            pltpu.VMEM((mid * hid, 9 * full * chans), BF16),
            pltpu.VMEM((9 * own, mid * hid), BF16),
            pltpu.VMEM((mid * hid, width), F32),
            pltpu.VMEM((own, area), F32),
            pltpu.VMEM((own, area), F32),
            pltpu.VMEM((3 * full * chans, padded), BF16),
            pltpu.VMEM((9 * own, padded), F32),
            pltpu.VMEM((own, area), F32),
            pltpu.VMEM((ITERS, own, area), BF16),
            pltpu.VMEM((ITERS, side, area), BF16),
            pltpu.VMEM((ITERS, side, area), BF16),
            pltpu.VMEM((ITERS - 1, own, area), BF16),
            pltpu.VMEM((ITERS - 1, own, area), BF16),
            pltpu.VMEM((ITERS - 1, own, area), BF16),
            pltpu.VMEM((ITERS - 1, own, area), BF16),
            pltpu.VMEM((own, area), F32),
            pltpu.VMEM((own, area), F32),
            pltpu.VMEM((own, area), F32),
            dma((ITERS, 2, chunks)),
            dma((ITERS, 2, chunks)),
            dma((ITERS, chunks)),
            dma((ITERS, chunks)),
            dma((ITERS, chunks)),
            dma((ITERS, chunks)),
        ],
        compiler_params=pltpu.CompilerParams(
            collective_id=0, has_side_effects=True, vmem_limit_bytes=48 * 1024 * 1024
        ),
    )(
        trajectory.reshape(flat, width),
        first_latent.reshape(flat, width),
        noise_draw.reshape(flat, width),
        jnp.transpose(w_in, (2, 3, 4, 1, 0)).reshape(27 * chans, hid),
        bias_in[None],
        level_bias,
        jnp.transpose(w_out, (2, 3, 4, 0, 1)).reshape(27 * chans, hid),
        bias_out[None],
        drift_coef,
        eps_coef,
        noise_coef,
    )
    return result.reshape(trajectory.shape)


def solution(mesh):
    placed = (
        P("level", None, "slab", None, None),
        P(None, "slab", None, None),
        P("level", None, "slab", None, None),
        P(),
        P(),
        P("level", None),
        P(),
        P(),
        P("level"),
        P("level"),
        P("level"),
    )
    return jax.shard_map(
        functools.partial(on_device, mesh.shape["level"], mesh.shape["slab"]),
        mesh=mesh,
        in_specs=placed,
        out_specs=P("level", None, "slab", None, None),
        check_vma=False,
    )
```

```python
import functools

import jax
import jax.numpy as jnp
from jax import lax
from jax.experimental import pallas as pl
from jax.experimental.pallas import tpu as pltpu
from jax.sharding import PartitionSpec as P

ITERS = 2
LAG = 5
MESH = pl.DeviceIdType.MESH
F32 = jnp.float32
BF16 = jnp.bfloat16


def kernel(
    dims,
    traj_hbm, first_hbm, noise_hbm, w_in_hbm, w_out_hbm,
    bias_in, level_bias, bias_out, drift, eps, nco,
    out,
    traj, first, noise, w_in, w_out, in_sem,
    a1, a2, bias_col, cur, base, xs, y, inc, sb, hl, hr, xsb, xr, zsb, zr, xr_last, zsb_last, zr_last,
    hs_sem, hr_sem, x_ssem, x_rsem, z_ssem, z_rsem,
):
    chans, hid, depth, rows, width, levels, slabs, chunk, block = dims
    level, slab = lax.axis_index("level"), lax.axis_index("slab")
    odd = lax.rem(level, 2)
    group = lax.div(level, 2)
    groups = levels // 2
    partner = level + 1 - 2 * odd
    stride = depth * rows
    own = depth * chans
    side = 2 * chans
    full = depth + 4
    mid = depth + 2
    chunks = rows // chunk
    lanes = lax.broadcasted_iota(jnp.int32, (1, width), 1)
    not_first = lanes > 0
    not_last = lanes < width - 1

    fetches = [
        pltpu.make_async_copy(src, dst, in_sem.at[i])
        for i, (src, dst) in enumerate((
            (traj_hbm, traj), (w_in_hbm, w_in), (w_out_hbm, w_out), (noise_hbm, noise), (first_hbm, first),
        ))
    ]
    for fetch in fetches:
        fetch.start()

    barrier = pltpu.get_barrier_semaphore()
    pl.semaphore_signal(barrier, inc=1, device_id={"level": partner}, device_id_type=MESH)

    @pl.when(group > 0)
    def _():
        pl.semaphore_signal(barrier, inc=1, device_id={"level": level - 2}, device_id_type=MESH)

    @pl.when(group < groups - 1)
    def _():
        pl.semaphore_signal(barrier, inc=1, device_id={"level": level + 2}, device_id_type=MESH)

    @pl.when(slab > 0)
    def _():
        pl.semaphore_signal(barrier, inc=1, device_id={"slab": slab - 1}, device_id_type=MESH)

    @pl.when(slab < slabs - 1)
    def _():
        pl.semaphore_signal(barrier, inc=1, device_id={"slab": slab + 1}, device_id_type=MESH)

    def one(cond):
        return jnp.where(cond, 1, 0)

    def rows_of(ref, h):
        return jnp.concatenate(
            [ref[pl.ds(d * rows + h, chans, stride=stride), :] for d in range(depth)], axis=0
        )

    def at(h, n=1, pad=0):
        return pl.ds(pl.multiple_of((h + pad) * width, width), n * width)

    fetches[0].wait()

    @pl.loop(0, chunks)
    def _(j):
        for r in range(chunk):
            h = j * chunk + r
            v = rows_of(traj, h)
            cur[:, at(h)] = v
            sb[0, :, at(h)] = v.astype(BF16)

    pl.semaphore_wait(
        barrier,
        1 + one(group > 0) + one(group < groups - 1) + one(slab > 0) + one(slab < slabs - 1),
    )

    def halo_copies(it, j, span):
        to_right = pltpu.make_async_remote_copy(
            src_ref=sb.at[it, pl.ds(own - side, side), span],
            dst_ref=hl.at[it, :, span],
            send_sem=hs_sem.at[it, 0, j],
            recv_sem=hr_sem.at[it, 0, j],
            device_id={"slab": slab + 1},
            device_id_type=MESH,
        )
        to_left = pltpu.make_async_remote_copy(
            src_ref=sb.at[it, pl.ds(0, side), span],
            dst_ref=hr.at[it, :, span],
            send_sem=hs_sem.at[it, 1, j],
            recv_sem=hr_sem.at[it, 1, j],
            device_id={"slab": slab - 1},
            device_id_type=MESH,
        )
        return to_right, to_left

    def halo_start(it, j):
        to_right, to_left = halo_copies(it, j, at(j * chunk, chunk))

        @pl.when(slab < slabs - 1)
        def _():
            to_right.start()

        @pl.when(slab > 0)
        def _():
            to_left.start()

    def halo_recv(it, j):
        to_right, to_left = halo_copies(it, j, at(j * chunk, chunk))

        @pl.when(slab > 0)
        def _():
            to_right.wait_recv()

        @pl.when(slab < slabs - 1)
        def _():
            to_left.wait_recv()

    def halo_sent(it, j):
        to_right, to_left = halo_copies(it, j, at(j * chunk, chunk))

        @pl.when(slab < slabs - 1)
        def _():
            to_right.wait_send()

        @pl.when(slab > 0)
        def _():
            to_left.wait_send()

    def wires(it):
        if it == ITERS - 1:
            return inc, xr_last, zsb_last, zr_last
        return xsb.at[it], xr.at[it], zsb.at[it], zr.at[it]

    def pair_copy(it, j):
        span = at(j * chunk, chunk)
        src, dst, _, _ = wires(it)
        return pltpu.make_async_remote_copy(
            src_ref=src.at[:, span],
            dst_ref=dst.at[:, span],
            send_sem=x_ssem.at[it, j],
            recv_sem=x_rsem.at[it, j],
            device_id={"level": partner},
            device_id_type=MESH,
        )

    def chain_copy(it, j):
        span = at(j * chunk, chunk)
        _, _, src, dst = wires(it)
        return pltpu.make_async_remote_copy(
            src_ref=src.at[:, span],
            dst_ref=dst.at[:, span],
            send_sem=z_ssem.at[it, j],
            recv_sem=z_rsem.at[it, j],
            device_id={"level": level + 2},
            device_id_type=MESH,
        )

    @pl.loop(0, chunks)
    def _(j):
        halo_start(0, j)

    @pl.when(slab == 0)
    def _():
        hl[...] = jnp.zeros_like(hl)

    @pl.when(slab == slabs - 1)
    def _():
        hr[...] = jnp.zeros_like(hr)

    @pl.when(group == 0)
    def _():
        zr[...] = jnp.zeros_like(zr)
        zr_last[...] = jnp.zeros_like(zr_last)

    for ref, dtype in ((xs, BF16), (y, F32)):
        n = ref.shape[0]
        ref[:, 0:width] = jnp.zeros((n, width), dtype)
        ref[:, (rows + 1) * width:(rows + 2) * width] = jnp.zeros((n, width), dtype)

    def tap(ref, n, kd, kh, kw):
        row = ((kd * 3 + kh) * 3 + kw) * n
        return ref[row:row + n, :]

    fetches[1].wait()
    fetches[2].wait()
    w_in, w_out = w_in[...].astype(F32), w_out[...].astype(F32)
    zero = jnp.zeros((chans, hid), F32)
    parts = []
    for kh in range(3):
        for kw in range(3):
            for q in range(full):
                parts.append(jnp.concatenate(
                    [tap(w_in, chans, q - p, kh, kw) if 0 <= q - p < 3 else zero for p in range(mid)],
                    axis=1,
                ))
    a1[...] = (0.5 * jnp.concatenate(parts, axis=0)).T.astype(BF16)

    keep = [jnp.float32(1.0)] * mid
    keep[0] = jnp.where(slab > 0, 1.0, 0.0).astype(F32)
    keep[-1] = jnp.where(slab < slabs - 1, 1.0, 0.0).astype(F32)
    parts = []
    for kh in range(3):
        for kw in range(3):
            for d in range(depth):
                parts.append(jnp.concatenate(
                    [tap(w_out, chans, p - d, kh, kw) * keep[p] if 0 <= p - d < 3 else zero for p in range(mid)],
                    axis=1,
                ))
    a2[...] = jnp.concatenate(parts, axis=0).astype(BF16)

    shift = jnp.broadcast_to(0.5 * (bias_in[...] + level_bias[...]), (width, hid)).T
    bias_col[...] = jnp.concatenate([shift] * mid, axis=0)
    tail = jnp.broadcast_to(bias_out[...] * eps[0], (width, chans)).T
    tail = jnp.concatenate([tail] * depth, axis=0)

    fetches[3].wait()

    @pl.loop(0, chunks)
    def _(j):
        for r in range(chunk):
            h = j * chunk + r
            base[:, at(h)] = rows_of(noise, h) * nco[0] + tail

    fetches[4].wait()
    drift_v, eps_v = drift[0], eps[0]

    for it in range(ITERS):
        last = it == ITERS - 1
        _, pair_in, chain_out, chain_in = wires(it)

        def build(j):
            halo_recv(it, j)
            for r in range(chunk):
                h = j * chunk + r
                v = jnp.concatenate(
                    [hl[it, :, at(h)], sb[it, :, at(h)], hr[it, :, at(h)]], axis=0
                ).astype(F32)
                n = full * chans
                xs[0:n, at(h, pad=1)] = jnp.where(not_first, pltpu.roll(v, 1, 1), 0.0).astype(BF16)
                xs[n:2 * n, at(h, pad=1)] = v.astype(BF16)
                xs[2 * n:3 * n, at(h, pad=1)] = jnp.where(
                    not_last, pltpu.roll(v, width - 1, 1), 0.0).astype(BF16)

        def convolve(b):
            h = b * block
            field = jnp.concatenate([xs[:, at(h, block, kh)] for kh in range(3)], axis=0)
            u = jnp.dot(a1[...], field, preferred_element_type=F32)
            u = u + jnp.concatenate([bias_col[...]] * block, axis=1)
            hidden = (u + u * jnp.tanh(u)).astype(BF16)
            y[:, at(h, block, 1)] = jnp.dot(a2[...], hidden, preferred_element_type=F32)

        def combine(j):
            for r in range(chunk):
                h = j * chunk + r
                taps = []
                for kw in range(3):
                    acc = None
                    for kh in range(3):
                        row = (kh * 3 + kw) * own
                        v = y[row:row + own, at(h, pad=kh)]
                        acc = v if acc is None else acc + v
                    taps.append(acc)
                pred = taps[1] + jnp.where(not_first, pltpu.roll(taps[0], 1, 1), 0.0)
                pred = pred + jnp.where(not_last, pltpu.roll(taps[2], width - 1, 1), 0.0)
                v = drift_v * cur[:, at(h)] + (eps_v * pred + base[:, at(h)])
                inc[:, at(h)] = v
                if not last:
                    xsb[it, :, at(h)] = v.astype(BF16)
            pair_copy(it, j).start()

        def scan(j):
            pair_copy(it, j).wait_recv()

            @pl.when(group > 0)
            def _():
                chain_copy(it, j).wait_recv()

            span = at(j * chunk, chunk)

            @pl.when(group < groups - 1)
            def _():
                total = chain_in[:, span].astype(F32) + (inc[:, span] + pair_in[:, span].astype(F32))
                chain_out[:, span] = total.astype(chain_out.dtype)
                chain_copy(it, j).start()

            odd_f = odd.astype(F32)
            for r in range(chunk):
                h = j * chunk + r
                v = rows_of(first, h) + (chain_in[:, at(h)].astype(F32) + odd_f * pair_in[:, at(h)].astype(F32))
                if last:
                    v = v + inc[:, at(h)]
                    for d in range(depth):
                        out[pl.ds(d * rows + h, chans, stride=stride), :] = v[d * chans:(d + 1) * chans]
                else:
                    cur[:, at(h)] = v
                    sb[it + 1, :, at(h)] = v.astype(BF16)
            if not last:
                halo_start(it + 1, j)

        @pl.loop(0, chunks + 2 + LAG)
        def _(step):
            for behind, stage in enumerate((build, convolve, combine)):
                @pl.when((step >= behind) & (step < chunks + behind))
                def _(stage=stage, behind=behind):
                    stage(step - behind)

            @pl.when(step >= 2 + LAG)
            def _():
                scan(step - 2 - LAG)

    @pl.loop(0, chunks)
    def _(j):
        for it in range(ITERS):
            halo_sent(it, j)
            pair_copy(it, j).wait_send()

            @pl.when(group < groups - 1)
            def _():
                chain_copy(it, j).wait_send()


def on_device(levels, slabs, trajectory, first_latent, noise_draw, w_in, bias_in, level_bias,
              w_out, bias_out, drift_coef, eps_coef, noise_coef):
    _, chans, depth, rows, width = trajectory.shape
    hid = w_in.shape[0]
    chunk = block = 4 if rows % 4 == 0 else rows
    chunks = rows // chunk
    own, side = depth * chans, 2 * chans
    full, mid = depth + 4, depth + 2
    area = rows * width
    padded = (rows + 2) * width
    flat = chans * depth * rows
    dims = (chans, hid, depth, rows, width, levels, slabs, chunk, block)
    vmem = pl.BlockSpec(memory_space=pltpu.VMEM)
    hbm = pl.BlockSpec(memory_space=pltpu.HBM)
    smem = pl.BlockSpec(memory_space=pltpu.SMEM)
    dma = pltpu.SemaphoreType.DMA
    result = pl.pallas_call(
        functools.partial(kernel, dims),
        out_shape=jax.ShapeDtypeStruct((flat, width), F32),
        in_specs=[hbm] * 5 + [vmem] * 3 + [smem] * 3,
        out_specs=vmem,
        scratch_shapes=[
            pltpu.VMEM((flat, width), F32),
            pltpu.VMEM((flat, width), F32),
            pltpu.VMEM((flat, width), F32),
            pltpu.VMEM((27 * chans, hid), BF16),
            pltpu.VMEM((27 * chans, hid), BF16),
            dma((5,)),
            pltpu.VMEM((mid * hid, 9 * full * chans), BF16),
            pltpu.VMEM((9 * own, mid * hid), BF16),
            pltpu.VMEM((mid * hid, width), F32),
            pltpu.VMEM((own, area), F32),
            pltpu.VMEM((own, area), F32),
            pltpu.VMEM((3 * full * chans, padded), BF16),
            pltpu.VMEM((9 * own, padded), F32),
            pltpu.VMEM((own, area), F32),
            pltpu.VMEM((ITERS, own, area), BF16),
            pltpu.VMEM((ITERS, side, area), BF16),
            pltpu.VMEM((ITERS, side, area), BF16),
            pltpu.VMEM((ITERS - 1, own, area), BF16),
            pltpu.VMEM((ITERS - 1, own, area), BF16),
            pltpu.VMEM((ITERS - 1, own, area), BF16),
            pltpu.VMEM((ITERS - 1, own, area), BF16),
            pltpu.VMEM((own, area), F32),
            pltpu.VMEM((own, area), F32),
            pltpu.VMEM((own, area), F32),
            dma((ITERS, 2, chunks)),
            dma((ITERS, 2, chunks)),
            dma((ITERS, chunks)),
            dma((ITERS, chunks)),
            dma((ITERS, chunks)),
            dma((ITERS, chunks)),
        ],
        compiler_params=pltpu.CompilerParams(
            collective_id=0, has_side_effects=True, vmem_limit_bytes=60 * 1024 * 1024
        ),
    )(
        trajectory.reshape(flat, width),
        first_latent.reshape(flat, width),
        noise_draw.reshape(flat, width),
        jnp.transpose(w_in, (2, 3, 4, 1, 0)).reshape(27 * chans, hid),
        jnp.transpose(w_out, (2, 3, 4, 0, 1)).reshape(27 * chans, hid),
        bias_in[None],
        level_bias,
        bias_out[None],
        drift_coef,
        eps_coef,
        noise_coef,
    )
    return result.reshape(trajectory.shape)


def solution(mesh):
    placed = (
        P("level", None, "slab", None, None),
        P(None, "slab", None, None),
        P("level", None, "slab", None, None),
        P(),
        P(),
        P("level", None),
        P(),
        P(),
        P("level"),
        P("level"),
        P("level"),
    )
    return jax.shard_map(
        functools.partial(on_device, mesh.shape["level"], mesh.shape["slab"]),
        mesh=mesh,
        in_specs=placed,
        out_specs=P("level", None, "slab", None, None),
        check_vma=False,
    )
```
